32 devices in a mesh: row: 8 (over y, x, core), col: 4 (over z).
Axes of the slice: x: 2, y: 2, z: 4, core: 2. Of those that a mesh axis runs over, the one named last changes fastest.
Arguments:
- out_grad: bfloat16 [512, 16384], P('col', 'row'), may hold values from -6 to 6
- gate_saved: bfloat16 [512, 26624], P('row', 'col'), may hold values from -8 to 8
- up_saved: bfloat16 [512, 26624], P('row', 'col'), may hold values from -6 to 6
- gate_weight: bfloat16 [16384, 26624], P('row', 'col'), may hold values from -0.046875 to 0.046875
- up_weight: bfloat16 [16384, 26624], P('row', 'col'), may hold values from -0.046875 to 0.046875
- down_weight: bfloat16 [26624, 16384], P('col', 'row'), may hold values from -0.0390625 to 0.0390625
Outputs:
- input_grad: bfloat16 [512, 16384], P('col', 'row')
The draws below stay inside these ranges and needn't reach their ends.
All inputs are finite; a program needn't handle non-finite values.
Results may differ from the reference program's by a relative error of at most 0.0049.
Values may be sent and summed in bfloat16 or wider, within the bound.
No kernel may reach another device: no remote copies, remote signals or barrier semaphores. Data moves between devices by JAX's collectives and lax.ppermute only.
A program may use at most 192 MiB of HBM per device.

```python
import jax
import jax.numpy as jnp

D = 16384
FF = 26624
TOKENS = 512


def level_of(own_key, extent, shards, smallest, largest):
    def one(position, blocks):
        draws = jax.random.uniform(jax.random.fold_in(jax.random.fold_in(own_key, 6), position), (blocks,), jnp.float32, smallest / len(shards), largest / len(shards))
        return jnp.repeat(jnp.exp(draws), extent[position] // blocks).reshape((-1,) + (1,) * (len(extent) - position - 1))

    level = one(*shards[0])
    for cut in shards[1:]:
        level = level * one(*cut)
    return level


def bell_draw(rng, extent, spread, most, split=(), dtype=jnp.bfloat16):
    entries = spread * jax.random.normal(rng, extent, jnp.float32)
    if split:
        entries = entries * level_of(rng, extent, split, -0.22, 0.18)
    return jnp.clip(entries, -most, most).astype(dtype)


def setup_inputs(seed: int = 0) -> dict:
    streams_of = jax.random.split(jax.random.key(seed), 7)
    return {
        "out_grad": bell_draw(streams_of[0], (TOKENS, D), 1.0, 6.0, ((0, 4), (1, 8))),
        "gate_saved": bell_draw(streams_of[1], (TOKENS, FF), 2.0, 8.0, ((0, 8), (1, 4))),
        "up_saved": bell_draw(streams_of[2], (TOKENS, FF), 1.0, 6.0, ((0, 8), (1, 4))),
        "gate_weight": bell_draw(streams_of[3], (D, FF), D ** -0.5, 0.046875, ((0, 8), (1, 4))),
        "up_weight": bell_draw(streams_of[4], (D, FF), D ** -0.5, 0.046875, ((0, 8), (1, 4))),
        "down_weight": bell_draw(streams_of[5], (FF, D), FF ** -0.5, 0.0390625, ((0, 4), (1, 8))),
    }


def reference(out_grad, gate_saved, up_saved, gate_weight, up_weight, down_weight):
    hidden_grad = jnp.dot(out_grad, down_weight.T, preferred_element_type=jnp.float32)
    gate_float = gate_saved.astype(jnp.float32)
    up_float = up_saved.astype(jnp.float32)
    sigmoid_gate = jax.nn.sigmoid(gate_float)
    up_grad = (hidden_grad * gate_float * sigmoid_gate).astype(jnp.bfloat16)
    gate_grad = (hidden_grad * up_float * sigmoid_gate * (1.0 + gate_float * (1.0 - sigmoid_gate))).astype(jnp.bfloat16)
    total = jnp.dot(gate_grad, gate_weight.T, preferred_element_type=jnp.float32)
    total = total + jnp.dot(up_grad, up_weight.T, preferred_element_type=jnp.float32)
    return total.astype(jnp.bfloat16)
```

```python
import jax
import jax.numpy as jnp
from jax import lax
from jax.sharding import PartitionSpec as P

TOKEN_CHUNKS = 2
HIDDEN_CHUNKS = 1


def contract_last(left, right):
    return lax.dot_general(
        left, right, (((1,), (1,)), ((), ())), preferred_element_type=jnp.float32
    )


def swiglu_back(hidden_grad, gate_saved, up_saved):
    gate_float = gate_saved.astype(jnp.float32)
    up_float = up_saved.astype(jnp.float32)
    sigmoid_gate = jax.nn.sigmoid(gate_float)
    up_grad = (hidden_grad * gate_float * sigmoid_gate).astype(jnp.bfloat16)
    gate_grad = (
        hidden_grad * up_float * sigmoid_gate * (1.0 + gate_float * (1.0 - sigmoid_gate))
    ).astype(jnp.bfloat16)
    return (gate_grad, up_grad)


def swap(value, axis, size, bit):
    return lax.ppermute(value, axis, [(i, i ^ bit) for i in range(size)])


def turn(value, axis, size, distance):
    return lax.ppermute(value, axis, [(i, (i + distance) % size) for i in range(size)])


def halve(blocks, rows, bits):
    state = dict(enumerate(blocks))
    for bit in bits:
        sent = [k for k in sorted(state) if k & bit]
        got = swap(
            jnp.stack([state[k] for k in sent]).astype(jnp.bfloat16), "row", rows, 2 * bit
        )
        for j, k in enumerate(sent):
            state[k ^ bit] = state[k ^ bit] + got[j].astype(jnp.float32)
            del state[k]
    return state[0]


def double(block, rows, bits):
    parts = [(block[None], [0])]
    for bit in bits:
        whole = parts[0][0] if len(parts) == 1 else jnp.concatenate([p for p, _ in parts])
        order = [k for _, ks in parts for k in ks]
        parts.append((swap(whole, "row", rows, 2 * bit), [k ^ bit for k in order]))
    placed = {k: p[j] for p, ks in parts for j, k in enumerate(ks)}
    return jnp.concatenate([placed[k] for k in sorted(placed)])


def per_device(rows, cols, out_grad, gate_saved, up_saved, gate_weight, up_weight, down_weight):
    me, plane = lax.axis_index("row"), lax.axis_index("col")
    share, hidden = gate_saved.shape
    width = out_grad.shape[1]
    per_plane = rows // cols
    step = share // TOKEN_CHUNKS
    depth = hidden // HIDDEN_CHUNKS
    half = rows // 2
    bits = [1 << i for i in range(half.bit_length() - 1)]
    order = [s for s in range(rows) if s & 1] + [s for s in range(rows) if not s & 1]
    back = [s for s in range(rows) if not s & 1] + [s for s in range(rows) if s & 1]

    results = []
    for t in range(TOKEN_CHUNKS):
        own = out_grad.reshape(per_plane, TOKEN_CHUNKS, step, width)[:, t]
        pieces = jnp.concatenate([own] + [turn(own, "col", cols, d) for d in range(1, cols)])
        picked = []
        for s in order:
            block = me ^ s
            far = lax.rem(plane - block // per_plane + cols, cols)
            picked.append(
                lax.dynamic_index_in_dim(
                    pieces, far * per_plane + lax.rem(block, per_plane), 0, keepdims=False
                )
            )
        tokens = jnp.concatenate(picked)
        total = None
        for h in range(HIDDEN_CHUNKS):
            span = slice(h * depth, (h + 1) * depth)
            partial = contract_last(tokens, down_weight[span]).astype(jnp.bfloat16)
            partial = partial.reshape(rows, step, depth)
            got = swap(partial[:half], "row", rows, 1)
            pair = partial[half:].astype(jnp.float32) + got.astype(jnp.float32)
            mid = depth // 2
            left = halve(list(pair[:, :, :mid]), rows, bits)
            right = halve(list(pair[:, :, mid:]), rows, bits[::-1])
            hidden_grad = jnp.concatenate([left, right], axis=1)
            mine = slice(t * step, (t + 1) * step)
            gate_grad, up_grad = swiglu_back(
                hidden_grad, gate_saved[mine, span], up_saved[mine, span]
            )
            gates = double(gate_grad, rows, bits)
            ups = double(up_grad, rows, bits[::-1])
            gates = jnp.concatenate([gates, swap(gates, "row", rows, 1)])
            ups = jnp.concatenate([ups, swap(ups, "row", rows, 1)])
            product = contract_last(gates, gate_weight[:, span]) + contract_last(
                ups, up_weight[:, span]
            )
            total = product if total is None else total + product
        total = total.reshape(rows, step, width)

        def owned_by(to):
            picked = []
            for sub in range(per_plane):
                s = me ^ (to * per_plane + sub)
                place = lax.rem(s, 2) * half + s // 2
                picked.append(lax.dynamic_index_in_dim(total, place, 0, keepdims=False))
            return jnp.stack(picked)

        result = owned_by(plane)
        for d in range(1, cols):
            sent = owned_by(lax.rem(plane + d, cols)).astype(jnp.bfloat16)
            result = result + turn(sent, "col", cols, d).astype(jnp.float32)
        results.append(result.astype(jnp.bfloat16))
    return jnp.stack(results, axis=1).reshape(out_grad.shape)


def solution(mesh):
    rows, cols = mesh.shape["row"], mesh.shape["col"]
    placed = (
        P("col", "row"),
        P("row", "col"),
        P("row", "col"),
        P("row", "col"),
        P("row", "col"),
        P("col", "row"),
    )

    def body(*arrays):
        return per_device(rows, cols, *arrays)

    return jax.shard_map(
        body, mesh=mesh, in_specs=placed, out_specs=P("col", "row"), check_vma=False
    )
```

```python
import functools

import jax
import jax.numpy as jnp
from jax import lax
from jax.experimental import pallas as pl
from jax.experimental.pallas import tpu as pltpu
from jax.sharding import PartitionSpec as P

TOKEN_CHUNKS = 2
SLOTS = 4
HINT = 1 << 10
MIB = 1 << 20


def contract_last(left, right):
    return lax.dot_general(
        left, right, (((1,), (1,)), ((), ())), preferred_element_type=jnp.float32
    )


def swiglu_back(hidden_grad, gate_saved, up_saved):
    gate_float = gate_saved.astype(jnp.float32)
    up_float = up_saved.astype(jnp.float32)
    sigmoid_gate = jax.nn.sigmoid(gate_float)
    up_grad = (hidden_grad * gate_float * sigmoid_gate).astype(jnp.bfloat16)
    gate_grad = (
        hidden_grad * up_float * sigmoid_gate * (1.0 + gate_float * (1.0 - sigmoid_gate))
    ).astype(jnp.bfloat16)
    return (gate_grad, up_grad)


def swap(value, size):
    return lax.ppermute(value, "row", [(i, i ^ 1) for i in range(size)])


def exchange(value, size, j):
    top = (size // 2).bit_length() - 2
    return lax.ppermute(
        value, "row", [(i, i ^ (2 << (top - j if i & 1 else j))) for i in range(size)]
    )


def turn(value, size, distance):
    return lax.ppermute(value, "col", [(i, (i + distance) % size) for i in range(size)])


def after(value, *earlier):
    return lax.optimization_barrier((value, *earlier))[0]


def flipped(chip, core, k, chips):
    other = 0
    count = chips.bit_length() - 1
    for i in range(count):
        flip = ((k >> i) & 1) + core * (((k >> (count - 1 - i)) & 1) - ((k >> i) & 1))
        other = other + ((chip // (1 << i)) % 2 + flip) % 2 * (1 << i)
    return other


def difference(chip, other, core, chips):
    k = 0
    count = chips.bit_length() - 1
    for i in range(count):
        differs = ((chip // (1 << i)) % 2 + (other // (1 << i)) % 2) % 2
        k = k + differs * ((1 << i) + core * ((1 << (count - 1 - i)) - (1 << i)))
    return k


def block_of(extent, most):
    return max(d for d in range(128, most + 1, 128) if extent % d == 0)


def hidden_kernel(rows, cols, starts, block, count, *refs):
    pieces, weight, refs = refs[:count], refs[count], refs[count + 1 :]
    outs, (tokens, buffer, sems) = refs[:-3], refs[-3:]
    me, plane = lax.axis_index("row"), lax.axis_index("col")
    per_plane, half = rows // cols, rows // 2
    step = outs[0].shape[1]
    steps = outs[0].shape[2] // block

    def fetch(start, i):
        slot = lax.rem(i, SLOTS)
        return pltpu.make_async_copy(
            weight.at[pl.ds(start + i * block, block)], buffer.at[slot], sems.at[slot]
        )

    for i in range(min(SLOTS, steps)):
        fetch(starts[0], i).start()

    def place(piece, owner_plane):
        for sub in range(per_plane):
            owner = owner_plane * per_plane + sub
            k = difference(me // 2, owner // 2, owner % 2, half)
            same = 1 - (owner % 2 + me % 2) % 2
            to = pl.multiple_of((same * half + k) * step, step)
            tokens[pl.ds(to, step), :] = piece[sub * step : (sub + 1) * step, :]

    place(pieces[0], plane)
    for d in range(1, cols):
        if count == cols:
            place(pieces[d], (plane + cols - d) % cols)
        else:
            pl.when(plane >= d)(functools.partial(place, pieces[d], plane - d))
            pl.when(plane + d < cols)(functools.partial(place, pieces[cols - 1 + d], plane + d))

    for n, start in enumerate(starts):
        send, keep = outs[2 * n : 2 * n + 2]
        if n:
            for i in range(min(SLOTS, steps)):
                fetch(start, i).start()

        def body(i, carry):
            fetch(start, i).wait()
            result = contract_last(tokens[...], buffer[lax.rem(i, SLOTS)])
            columns = pl.ds(pl.multiple_of(i * block, 128), block)
            for k in range(half):
                send[k, :, columns] = result[k * step : (k + 1) * step].astype(send.dtype)
                keep[k, :, columns] = result[(half + k) * step : (half + k + 1) * step]

            @pl.when(i + SLOTS < steps)
            def _():
                fetch(start, i + SLOTS).start()

            return carry

        lax.fori_loop(0, steps, body, 0)


def hidden_partial(rows, cols, pieces, weight, starts, size):
    count, width = pieces[0].shape
    step = count * cols // rows
    half = rows // 2
    block = block_of(size, 256)
    whole = pl.BlockSpec(memory_space=pltpu.VMEM)
    return pl.pallas_call(
        functools.partial(hidden_kernel, rows, cols, starts, block, len(pieces)),
        out_shape=(
            jax.ShapeDtypeStruct((half, step, size), jnp.bfloat16),
            jax.ShapeDtypeStruct((half, step, size), jnp.float32),
        )
        * len(starts),
        in_specs=[whole] * len(pieces) + [pl.BlockSpec(memory_space=pl.ANY)],
        out_specs=(whole,) * (2 * len(starts)),
        scratch_shapes=[
            pltpu.VMEM((rows * step, width), jnp.bfloat16),
            pltpu.VMEM((SLOTS, block, width), jnp.bfloat16),
            pltpu.SemaphoreType.DMA((SLOTS,)),
        ],
        compiler_params=pltpu.CompilerParams(vmem_limit_bytes=40 * MIB),
        cost_estimate=pl.CostEstimate(flops=HINT, bytes_accessed=HINT, transcendentals=0),
    )(*pieces, weight)


def input_kernel(rows, cols, start, block, *refs):
    pieces, gate_weight, up_weight = refs[:rows], refs[rows], refs[rows + 1]
    outs, (left, right, buffer, sems) = refs[rows + 2 : -4], refs[-4:]
    me, plane = lax.axis_index("row"), lax.axis_index("col")
    per_plane, half = rows // cols, rows // 2
    step, depth = pieces[0].shape[1:]
    steps = outs[0].shape[1] // block
    count = per_plane * step

    def fetch(which, i):
        slot = lax.rem(2 * i + which, SLOTS)
        return pltpu.make_async_copy(
            (gate_weight, up_weight)[which].at[pl.ds(start + i * block, block)],
            buffer.at[slot],
            sems.at[slot],
        )

    for i in range(min(SLOTS, 2 * steps)):
        fetch(i % 2, i // 2).start()
    for j, piece in enumerate(pieces):
        core = (me + j // half) % 2
        owner = 2 * flipped(me // 2, core, j % half, half) + core
        distance = (owner // per_plane + cols - plane) % cols
        place = pl.multiple_of((distance * per_plane + owner % per_plane) * step, step)
        left[pl.ds(place, step), :] = piece[0]
        right[pl.ds(place, step), :] = piece[1]

    def multiply(which, held, i):
        fetch(which, i).wait()
        product = contract_last(held[...], buffer[lax.rem(2 * i + which, SLOTS)])

        @pl.when(2 * i + which + SLOTS < 2 * steps)
        def _():
            fetch(which, i + SLOTS // 2).start()

        return product

    def body(i, carry):
        result = multiply(0, left, i) + multiply(1, right, i)
        columns = pl.ds(pl.multiple_of(i * block, 128), block)
        outs[0][:, columns] = result[:count]
        for d in range(1, cols):
            outs[d][:, columns] = result[d * count : (d + 1) * count].astype(jnp.bfloat16)
        return carry

    lax.fori_loop(0, steps, body, 0)


def input_partial(rows, cols, pieces, gate_weight, up_weight, start, size):
    _, step, depth = pieces[0].shape
    count = step * rows // cols
    block = block_of(size, 256)
    whole, anywhere = pl.BlockSpec(memory_space=pltpu.VMEM), pl.BlockSpec(memory_space=pl.ANY)
    return pl.pallas_call(
        functools.partial(input_kernel, rows, cols, start, block),
        out_shape=(jax.ShapeDtypeStruct((count, size), jnp.float32),)
        + (jax.ShapeDtypeStruct((count, size), jnp.bfloat16),) * (cols - 1),
        in_specs=[whole] * rows + [anywhere] * 2,
        out_specs=(whole,) * cols,
        scratch_shapes=[
            pltpu.VMEM((rows * step, depth), jnp.bfloat16),
            pltpu.VMEM((rows * step, depth), jnp.bfloat16),
            pltpu.VMEM((SLOTS, block, depth), jnp.bfloat16),
            pltpu.SemaphoreType.DMA((SLOTS,)),
        ],
        compiler_params=pltpu.CompilerParams(vmem_limit_bytes=40 * MIB),
        cost_estimate=pl.CostEstimate(flops=HINT, bytes_accessed=HINT, transcendentals=0),
    )(*pieces, gate_weight, up_weight)


class Chain:
    def __init__(self):
        self.last = []

    def begin(self, value):
        return after(value, *self.last) if self.last else value

    def end(self, *values):
        self.last = list(values)


class Halving:
    def __init__(self, chain, rows, send, keep):
        self.chain, self.rows, self.keep = chain, rows, keep
        self.got, self.step = swap(send, rows), 0

    def pair(self):
        got = self.chain.begin(self.got)
        pair = self.keep + got.astype(jnp.float32)
        self.state = {k: pair[k] for k in range(pair.shape[0])}
        self.send()

    def send(self):
        self.sent = [k for k in sorted(self.state) if (k >> self.step) & 1]
        value = jnp.stack([self.state[k] for k in self.sent]).astype(jnp.bfloat16)
        self.chain.end(value)
        self.got = exchange(value, self.rows, self.step)

    def add(self):
        got = self.chain.begin(self.got)
        for j, k in enumerate(self.sent):
            to = k ^ (1 << self.step)
            self.state[to] = self.state[to] + got[j].astype(jnp.float32)
            del self.state[k]
        self.step += 1


def per_device(rows, cols, out_grad, gate_saved, up_saved, gate_weight, up_weight, down_weight):
    share, hidden = gate_saved.shape
    width = out_grad.shape[1]
    per_plane = rows // cols
    step = share // TOKEN_CHUNKS
    mid = hidden // 2
    half = rows // 2
    bits = range(half.bit_length() - 1)
    chain = Chain()

    def tokens(t):
        own = out_grad.reshape(per_plane, TOKEN_CHUNKS, step, width)[:, t]
        return own.reshape(per_plane * step, width)

    def multiply(pieces, parts):
        pieces = [chain.begin(pieces[0])] + pieces[1:]
        outs = hidden_partial(rows, cols, pieces, down_weight, [i * mid for i in parts], mid)
        chain.end(outs[1])
        return [
            Halving(chain, rows, *outs[2 * n : 2 * n + 2]) for n in range(len(parts))
        ]

    def next_sums(sides):
        for side in sides:
            side.add()
            side.send()

    def activate(t, sides):
        for side in sides:
            side.add()
        hidden_grad = jnp.concatenate([side.state[0] for side in sides], axis=1)
        mine = slice(t * step, (t + 1) * step)
        both = jnp.stack(swiglu_back(hidden_grad, gate_saved[mine], up_saved[mine]))
        chain.end(both)
        return [both]

    def spread(pieces):
        j = len(pieces).bit_length() - 1
        return pieces + [exchange(piece, rows, j) for piece in pieces]

    def cross(pieces):
        return pieces + [swap(piece, rows) for piece in pieces]

    def share_of(pieces, start, size):
        pieces = [chain.begin(pieces[0])] + pieces[1:]
        outs = input_partial(rows, cols, pieces, gate_weight, up_weight, start, size)
        chain.end(outs[0])
        return outs

    def start_sums(own, *sends):
        return [own] + [turn(send, cols, d) for d, send in enumerate(sends, 1)]

    def finish_sums(own, *others):
        own = chain.begin(own)
        for other in others:
            own = own + other.astype(jnp.float32)
        own = own.astype(jnp.bfloat16)
        chain.end(own)
        return own

    own, later = tokens(0), tokens(1)
    near = [own] + [turn(own, cols, d) for d in range(1, cols)]
    later = after(later, near[1])
    far = [later] + [turn(later, cols, d) for d in range(1, cols)]

    first = multiply(near, [0]) + multiply(near, [1])
    for side in first:
        side.pair()
    for _ in bits[1:]:
        next_sums(first)
    second = multiply(far, [0])
    first = activate(0, first)
    for _ in bits:
        first = spread(first)
    second += multiply(far, [1])
    for side in second:
        side.pair()
    for _ in bits[1:]:
        next_sums(second)
    chain.last += first[1:]
    second = activate(1, second)
    for _ in bits[1:]:
        second = spread(second)
    first = cross(first)
    sums = [share_of(first, 0, width // 2)]
    second = [chain.begin(piece) if j else piece for j, piece in enumerate(second)]
    second = spread(second)
    sums.append(share_of(first, width // 2, width // 2))
    sums = start_sums(*[jnp.concatenate(some, axis=1) for some in zip(*sums)])
    second = cross(second)
    results = [start_sums(*share_of(second, 0, width // 2))]
    first = finish_sums(*sums)
    results.append(start_sums(*share_of(second, width // 2, width // 2)))
    second = jnp.concatenate([finish_sums(*some) for some in results], axis=1)
    results = [value.reshape(per_plane, step, width) for value in (first, second)]
    return jnp.stack(results, axis=1).reshape(out_grad.shape)


def solution(mesh):
    rows, cols = mesh.shape["row"], mesh.shape["col"]
    placed = (
        P("col", "row"),
        P("row", "col"),
        P("row", "col"),
        P("row", "col"),
        P("row", "col"),
        P("col", "row"),
    )
    return jax.shard_map(
        functools.partial(per_device, rows, cols),
        mesh=mesh,
        in_specs=placed,
        out_specs=P("col", "row"),
        check_vma=False,
    )
```

```python
import functools

import jax
import jax.numpy as jnp
from jax import lax
from jax.experimental import pallas as pl
from jax.experimental.pallas import tpu as pltpu
from jax.sharding import PartitionSpec as P

TOKEN_CHUNKS = 2
SLOTS = 4
HINT = 1 << 10
MIB = 1 << 20


def contract_last(left, right):
    return lax.dot_general(
        left, right, (((1,), (1,)), ((), ())), preferred_element_type=jnp.float32
    )


def swiglu_back(hidden_grad, gate_saved, up_saved):
    gate_float = gate_saved.astype(jnp.float32)
    up_float = up_saved.astype(jnp.float32)
    sigmoid_gate = jax.nn.sigmoid(gate_float)
    up_grad = (hidden_grad * gate_float * sigmoid_gate).astype(jnp.bfloat16)
    gate_grad = (
        hidden_grad * up_float * sigmoid_gate * (1.0 + gate_float * (1.0 - sigmoid_gate))
    ).astype(jnp.bfloat16)
    return (gate_grad, up_grad)


def swap(value, size):
    return lax.ppermute(value, "row", [(i, i ^ 1) for i in range(size)])


def exchange(value, size, j):
    top = (size // 2).bit_length() - 2
    return lax.ppermute(
        value, "row", [(i, i ^ (2 << (top - j if i & 1 else j))) for i in range(size)]
    )


def turn(value, size, distance):
    return lax.ppermute(value, "col", [(i, (i + distance) % size) for i in range(size)])


def after(value, *earlier):
    return lax.optimization_barrier((value, *earlier))[0]


def flipped(chip, core, k, chips):
    other = 0
    count = chips.bit_length() - 1
    for i in range(count):
        flip = ((k >> i) & 1) + core * (((k >> (count - 1 - i)) & 1) - ((k >> i) & 1))
        other = other + ((chip // (1 << i)) % 2 + flip) % 2 * (1 << i)
    return other


def difference(chip, other, core, chips):
    k = 0
    count = chips.bit_length() - 1
    for i in range(count):
        differs = ((chip // (1 << i)) % 2 + (other // (1 << i)) % 2) % 2
        k = k + differs * ((1 << i) + core * ((1 << (count - 1 - i)) - (1 << i)))
    return k


def block_of(extent, most):
    return max(d for d in range(128, most + 1, 128) if extent % d == 0)


def hidden_kernel(rows, cols, starts, block, count, *refs):
    pieces, weight, refs = refs[:count], refs[count], refs[count + 1 :]
    outs, (tokens, buffer, sems) = refs[:-3], refs[-3:]
    me, plane = lax.axis_index("row"), lax.axis_index("col")
    per_plane, half = rows // cols, rows // 2
    step = outs[0].shape[1]
    steps = outs[0].shape[2] // block

    def fetch(start, i):
        slot = lax.rem(i, SLOTS)
        return pltpu.make_async_copy(
            weight.at[pl.ds(start + i * block, block)], buffer.at[slot], sems.at[slot]
        )

    for i in range(min(SLOTS, steps)):
        fetch(starts[0], i).start()

    def place(piece, owner_plane):
        for sub in range(per_plane):
            owner = owner_plane * per_plane + sub
            k = difference(me // 2, owner // 2, owner % 2, half)
            same = 1 - (owner % 2 + me % 2) % 2
            to = pl.multiple_of((same * half + k) * step, step)
            tokens[pl.ds(to, step), :] = piece[sub * step : (sub + 1) * step, :]

    place(pieces[0], plane)
    for d in range(1, cols):
        if count == cols:
            place(pieces[d], (plane + cols - d) % cols)
        else:
            pl.when(plane >= d)(functools.partial(place, pieces[d], plane - d))
            pl.when(plane + d < cols)(functools.partial(place, pieces[cols - 1 + d], plane + d))

    for n, start in enumerate(starts):
        send, keep = outs[2 * n : 2 * n + 2]
        if n:
            for i in range(min(SLOTS, steps)):
                fetch(start, i).start()

        def body(i, carry):
            fetch(start, i).wait()
            result = contract_last(tokens[...], buffer[lax.rem(i, SLOTS)])
            columns = pl.ds(pl.multiple_of(i * block, 128), block)
            for k in range(half):
                send[k, :, columns] = result[k * step : (k + 1) * step].astype(send.dtype)
                keep[k, :, columns] = result[(half + k) * step : (half + k + 1) * step]

            @pl.when(i + SLOTS < steps)
            def _():
                fetch(start, i + SLOTS).start()

            return carry

        lax.fori_loop(0, steps, body, 0)


def hidden_partial(rows, cols, pieces, weight, starts, size):
    count, width = pieces[0].shape
    step = count * cols // rows
    half = rows // 2
    block = block_of(size, 256)
    whole = pl.BlockSpec(memory_space=pltpu.VMEM)
    return pl.pallas_call(
        functools.partial(hidden_kernel, rows, cols, starts, block, len(pieces)),
        out_shape=(
            jax.ShapeDtypeStruct((half, step, size), jnp.bfloat16),
            jax.ShapeDtypeStruct((half, step, size), jnp.float32),
        )
        * len(starts),
        in_specs=[whole] * len(pieces) + [pl.BlockSpec(memory_space=pl.ANY)],
        out_specs=(whole,) * (2 * len(starts)),
        scratch_shapes=[
            pltpu.VMEM((rows * step, width), jnp.bfloat16),
            pltpu.VMEM((SLOTS, block, width), jnp.bfloat16),
            pltpu.SemaphoreType.DMA((SLOTS,)),
        ],
        compiler_params=pltpu.CompilerParams(vmem_limit_bytes=39 * MIB),
        cost_estimate=pl.CostEstimate(flops=HINT, bytes_accessed=HINT, transcendentals=0),
    )(*pieces, weight)


def input_kernel(rows, cols, start, block, *refs):
    refs, (buffer, sems) = refs[:-2], refs[-2:]
    given = len(refs) - 2 - cols
    whole = given == 2
    if whole:
        (left, right), refs = refs[:2], refs[2:]
    else:
        given -= 2
        pieces, refs, (left, right) = refs[:given], refs[given:-2], refs[-2:]
    (gate_weight, up_weight), outs = refs[:2], refs[2:]
    me, plane = lax.axis_index("row"), lax.axis_index("col")
    per_plane, half = rows // cols, rows // 2
    depth = left.shape[1]
    step = left.shape[0] // rows
    steps = outs[0].shape[1] // block
    count = per_plane * step

    def fetch(which, i):
        slot = lax.rem(2 * i + which, SLOTS)
        return pltpu.make_async_copy(
            (gate_weight, up_weight)[which].at[pl.ds(start + i * block, block)],
            buffer.at[slot],
            sems.at[slot],
        )

    for i in range(min(SLOTS, 2 * steps)):
        fetch(i % 2, i // 2).start()
    places = []
    for j in range(rows):
        core = (me + j // half) % 2
        owner = 2 * flipped(me // 2, core, j % half, half) + core
        distance = (owner // per_plane + cols - plane) % cols
        places.append(pl.multiple_of((distance * per_plane + owner % per_plane) * step, step))
    if not whole and given == rows:
        for piece, place in zip(pieces, places):
            left[pl.ds(place, step), :] = piece[0]
            right[pl.ds(place, step), :] = piece[1]
    elif not whole:
        some = block_of(depth, 512)

        def activate(i, carry):
            columns = pl.ds(pl.multiple_of(i * some, 128), some)
            for hidden_grad, saved, place in zip(pieces[:rows], pieces[rows:], places):
                gate_grad, up_grad = swiglu_back(
                    hidden_grad[:, columns].astype(jnp.float32),
                    saved[0, :, columns],
                    saved[1, :, columns],
                )
                left[pl.ds(place, step), columns] = gate_grad
                right[pl.ds(place, step), columns] = up_grad
            return carry

        lax.fori_loop(0, depth // some, activate, 0)

    def multiply(which, held, i):
        fetch(which, i).wait()
        product = contract_last(held[...], buffer[lax.rem(2 * i + which, SLOTS)])

        @pl.when(2 * i + which + SLOTS < 2 * steps)
        def _():
            fetch(which, i + SLOTS // 2).start()

        return product

    def body(i, carry):
        result = multiply(0, left, i) + multiply(1, right, i)
        columns = pl.ds(pl.multiple_of(i * block, 128), block)
        outs[0][:, columns] = result[:count]
        for d in range(1, cols):
            outs[d][:, columns] = result[d * count : (d + 1) * count].astype(jnp.bfloat16)
        return carry

    lax.fori_loop(0, steps, body, 0)


def input_partial(rows, cols, given, gate_weight, up_weight, start, size):
    step, depth = given[0].shape[-2:]
    if len(given) == 2:
        step //= rows
    count = step * rows // cols
    block = block_of(size, 256)
    whole, anywhere = pl.BlockSpec(memory_space=pltpu.VMEM), pl.BlockSpec(memory_space=pl.ANY)
    outs = (jax.ShapeDtypeStruct((count, size), jnp.float32),)
    outs += (jax.ShapeDtypeStruct((count, size), jnp.bfloat16),) * (cols - 1)
    if len(given) > 2:
        outs += (jax.ShapeDtypeStruct((rows * step, depth), jnp.bfloat16),) * 2
    outs = pl.pallas_call(
        functools.partial(input_kernel, rows, cols, start, block),
        out_shape=outs,
        in_specs=[whole] * len(given) + [anywhere] * 2,
        out_specs=(whole,) * len(outs),
        scratch_shapes=[
            pltpu.VMEM((SLOTS, block, depth), jnp.bfloat16),
            pltpu.SemaphoreType.DMA((SLOTS,)),
        ],
        compiler_params=pltpu.CompilerParams(vmem_limit_bytes=39 * MIB),
        cost_estimate=pl.CostEstimate(flops=HINT, bytes_accessed=HINT, transcendentals=0),
    )(*given, gate_weight, up_weight)
    return outs[:cols], outs[cols:]


class Chain:
    def __init__(self):
        self.last = []

    def begin(self, value):
        return after(value, *self.last) if self.last else value

    def end(self, *values):
        self.last = list(values)


class Halving:
    def __init__(self, chain, rows, send, keep):
        self.chain, self.rows, self.keep = chain, rows, keep
        self.got, self.step = swap(send, rows), 0

    def pair(self):
        got = self.chain.begin(self.got)
        pair = self.keep + got.astype(jnp.float32)
        self.state = {k: pair[k] for k in range(pair.shape[0])}
        self.send()

    def send(self):
        self.sent = [k for k in sorted(self.state) if (k >> self.step) & 1]
        value = jnp.stack([self.state[k] for k in self.sent]).astype(jnp.bfloat16)
        self.chain.end(value)
        self.got = exchange(value, self.rows, self.step)

    def add(self):
        got = self.chain.begin(self.got)
        for j, k in enumerate(self.sent):
            to = k ^ (1 << self.step)
            self.state[to] = self.state[to] + got[j].astype(jnp.float32)
            del self.state[k]
        self.step += 1


def per_device(rows, cols, out_grad, gate_saved, up_saved, gate_weight, up_weight, down_weight):
    share, hidden = gate_saved.shape
    width = out_grad.shape[1]
    per_plane = rows // cols
    step = share // TOKEN_CHUNKS
    mid = hidden // 2
    half = rows // 2
    bits = range(half.bit_length() - 1)
    chain = Chain()

    def tokens(t):
        own = out_grad.reshape(per_plane, TOKEN_CHUNKS, step, width)[:, t]
        return own.reshape(per_plane * step, width)

    def multiply(pieces, parts):
        pieces = [chain.begin(pieces[0])] + pieces[1:]
        outs = hidden_partial(rows, cols, pieces, down_weight, [i * mid for i in parts], mid)
        chain.end(outs[1])
        return [
            Halving(chain, rows, *outs[2 * n : 2 * n + 2]) for n in range(len(parts))
        ]

    def next_sums(sides):
        for side in sides:
            side.add()
            side.send()

    def own_hidden(sides):
        for side in sides:
            side.add()
        return jnp.concatenate([side.state[0] for side in sides], axis=1)

    def saved(t):
        mine = slice(t * step, (t + 1) * step)
        return gate_saved[mine], up_saved[mine]

    def spread(pieces):
        j = len(pieces).bit_length() - 1
        return pieces + [exchange(piece, rows, j) for piece in pieces]

    def cross(pieces):
        return pieces + [swap(piece, rows) for piece in pieces]

    def share_of(given, start, size):
        given = [chain.begin(given[0])] + list(given[1:])
        outs, both = input_partial(rows, cols, given, gate_weight, up_weight, start, size)
        chain.end(outs[0])
        return outs, both

    def start_sums(own, *sends):
        return [own] + [turn(send, cols, d) for d, send in enumerate(sends, 1)]

    def add_up(own, *others):
        own = chain.begin(own)
        for other in others:
            own = own + other.astype(jnp.float32)
        chain.end(own)
        return own

    own, later = tokens(0), tokens(1)
    near = [own] + [turn(own, cols, d) for d in range(1, cols)]
    later = after(later, near[1])
    far = [later] + [turn(later, cols, d) for d in range(1, cols)]

    known = [jnp.stack(saved(0))]
    for _ in bits[1:]:
        known = spread(known)
    chain.end(*known[1:])
    first = multiply(near, [0])
    known = spread(known)
    chain.last += known[1:]
    first += multiply(near, [1])
    known = cross(known)
    for side in first:
        side.pair()
    chain.last += known[1:]
    for _ in bits[1:]:
        next_sums(first)
    second = multiply(far, [0])
    first = [own_hidden(first).astype(jnp.bfloat16)]
    chain.end(first[0])
    for _ in bits:
        first = spread(first)
    second += multiply(far, [1])
    for side in second:
        side.pair()
    for _ in bits[1:]:
        next_sums(second)
    chain.last += first[1:]
    second = [jnp.stack(swiglu_back(own_hidden(second), *saved(1)))]
    chain.end(second[0])
    for _ in bits[1:]:
        second = spread(second)
    first = cross(first)
    sums, both = share_of(first + known, 0, width // 2)
    second = [chain.begin(piece) if j else piece for j, piece in enumerate(second)]
    second = spread(second)
    rest, _ = share_of(both, width // 2, width // 2)
    first = start_sums(*[jnp.concatenate(some, axis=1) for some in zip(sums, rest)])
    second = cross(second)
    sums, both = share_of(second, 0, width // 2)
    second = [start_sums(*sums)]
    first = [add_up(*first[:2])] + first[2:]
    sums, _ = share_of(both, width // 2, width // 2)
    first = add_up(*first).astype(jnp.bfloat16)
    second.append(start_sums(*sums))
    second = jnp.concatenate([add_up(*some).astype(jnp.bfloat16) for some in second], axis=1)
    results = [value.reshape(per_plane, step, width) for value in (first, second)]
    return jnp.stack(results, axis=1).reshape(out_grad.shape)


def solution(mesh):
    rows, cols = mesh.shape["row"], mesh.shape["col"]
    placed = (
        P("col", "row"),
        P("row", "col"),
        P("row", "col"),
        P("row", "col"),
        P("row", "col"),
        P("col", "row"),
    )
    return jax.shard_map(
        functools.partial(per_device, rows, cols),
        mesh=mesh,
        in_specs=placed,
        out_specs=P("col", "row"),
        check_vma=False,
    )
```

```python
import functools

import jax
import jax.numpy as jnp
from jax import lax
from jax.experimental import pallas as pl
from jax.experimental.pallas import tpu as pltpu
from jax.sharding import PartitionSpec as P

TOKEN_CHUNKS = 2
SLOTS = 4
HINT = 1 << 10
MIB = 1 << 20


def contract_last(left, right):
    return lax.dot_general(
        left, right, (((1,), (1,)), ((), ())), preferred_element_type=jnp.float32
    )


def swiglu_back(hidden_grad, gate_saved, up_saved):
    gate_float = gate_saved.astype(jnp.float32)
    up_float = up_saved.astype(jnp.float32)
    sigmoid_gate = jax.nn.sigmoid(gate_float)
    up_grad = (hidden_grad * gate_float * sigmoid_gate).astype(jnp.bfloat16)
    gate_grad = (
        hidden_grad * up_float * sigmoid_gate * (1.0 + gate_float * (1.0 - sigmoid_gate))
    ).astype(jnp.bfloat16)
    return (gate_grad, up_grad)


def swap(value, size):
    return lax.ppermute(value, "row", [(i, i ^ 1) for i in range(size)])


def exchange(value, size, j):
    top = (size // 2).bit_length() - 2
    return lax.ppermute(
        value, "row", [(i, i ^ (2 << (top - j if i & 1 else j))) for i in range(size)]
    )


def turn(value, size, distance):
    return lax.ppermute(value, "col", [(i, (i + distance) % size) for i in range(size)])


def after(value, *earlier):
    return lax.optimization_barrier((value, *earlier))[0]


def flipped(chip, core, k, chips):
    other = 0
    count = chips.bit_length() - 1
    for i in range(count):
        flip = ((k >> i) & 1) + core * (((k >> (count - 1 - i)) & 1) - ((k >> i) & 1))
        other = other + ((chip // (1 << i)) % 2 + flip) % 2 * (1 << i)
    return other


def difference(chip, other, core, chips):
    k = 0
    count = chips.bit_length() - 1
    for i in range(count):
        differs = ((chip // (1 << i)) % 2 + (other // (1 << i)) % 2) % 2
        k = k + differs * ((1 << i) + core * ((1 << (count - 1 - i)) - (1 << i)))
    return k


def block_of(extent, most):
    return max(d for d in range(128, most + 1, 128) if extent % d == 0)


def hidden_kernel(rows, cols, starts, block, count, *refs):
    pieces, weight, refs = refs[:count], refs[count], refs[count + 1 :]
    outs, (tokens, buffer, sems) = refs[:-3], refs[-3:]
    me, plane = lax.axis_index("row"), lax.axis_index("col")
    per_plane, half = rows // cols, rows // 2
    step = outs[0].shape[1]
    steps = outs[0].shape[2] // block

    def fetch(start, i):
        slot = lax.rem(i, SLOTS)
        return pltpu.make_async_copy(
            weight.at[pl.ds(start + i * block, block)], buffer.at[slot], sems.at[slot]
        )

    for i in range(min(SLOTS, steps)):
        fetch(starts[0], i).start()

    def place(piece, owner_plane):
        for sub in range(per_plane):
            owner = owner_plane * per_plane + sub
            k = difference(me // 2, owner // 2, owner % 2, half)
            same = 1 - (owner % 2 + me % 2) % 2
            to = pl.multiple_of((same * half + k) * step, step)
            tokens[pl.ds(to, step), :] = piece[sub * step : (sub + 1) * step, :]

    place(pieces[0], plane)
    for d in range(1, cols):
        if count == cols:
            place(pieces[d], (plane + cols - d) % cols)
        else:
            pl.when(plane >= d)(functools.partial(place, pieces[d], plane - d))
            pl.when(plane + d < cols)(functools.partial(place, pieces[cols - 1 + d], plane + d))

    for n, start in enumerate(starts):
        send, keep = outs[2 * n : 2 * n + 2]
        if n:
            for i in range(min(SLOTS, steps)):
                fetch(start, i).start()

        def body(i, carry):
            fetch(start, i).wait()
            result = contract_last(tokens[...], buffer[lax.rem(i, SLOTS)])
            columns = pl.ds(pl.multiple_of(i * block, 128), block)
            for k in range(half):
                send[k, :, columns] = result[k * step : (k + 1) * step].astype(send.dtype)
                keep[k, :, columns] = result[(half + k) * step : (half + k + 1) * step]

            @pl.when(i + SLOTS < steps)
            def _():
                fetch(start, i + SLOTS).start()

            return carry

        lax.fori_loop(0, steps, body, 0)


def hidden_partial(rows, cols, pieces, weight, starts, size):
    count, width = pieces[0].shape
    step = count * cols // rows
    half = rows // 2
    block = block_of(size, 256)
    whole = pl.BlockSpec(memory_space=pltpu.VMEM)
    return pl.pallas_call(
        functools.partial(hidden_kernel, rows, cols, starts, block, len(pieces)),
        out_shape=(
            jax.ShapeDtypeStruct((half, step, size), jnp.bfloat16),
            jax.ShapeDtypeStruct((half, step, size), jnp.float32),
        )
        * len(starts),
        in_specs=[whole] * len(pieces) + [pl.BlockSpec(memory_space=pl.ANY)],
        out_specs=(whole,) * (2 * len(starts)),
        scratch_shapes=[
            pltpu.VMEM((rows * step, width), jnp.bfloat16),
            pltpu.VMEM((SLOTS, block, width), jnp.bfloat16),
            pltpu.SemaphoreType.DMA((SLOTS,)),
        ],
        compiler_params=pltpu.CompilerParams(vmem_limit_bytes=39 * MIB),
        cost_estimate=pl.CostEstimate(flops=HINT, bytes_accessed=HINT, transcendentals=0),
    )(*pieces, weight)


def input_kernel(rows, cols, start, block, *refs):
    refs, (buffer, sems) = refs[:-2], refs[-2:]
    given = len(refs) - 2 - cols
    whole = given == 2
    if whole:
        (left, right), refs = refs[:2], refs[2:]
    else:
        given -= 2
        pieces, refs, (left, right) = refs[:given], refs[given:-2], refs[-2:]
    (gate_weight, up_weight), outs = refs[:2], refs[2:]
    me, plane = lax.axis_index("row"), lax.axis_index("col")
    per_plane, half = rows // cols, rows // 2
    depth = left.shape[1]
    step = left.shape[0] // rows
    steps = outs[0].shape[1] // block
    count = per_plane * step

    def fetch(which, i):
        slot = lax.rem(2 * i + which, SLOTS)
        return pltpu.make_async_copy(
            (gate_weight, up_weight)[which].at[pl.ds(start + i * block, block)],
            buffer.at[slot],
            sems.at[slot],
        )

    for i in range(min(SLOTS, 2 * steps)):
        fetch(i % 2, i // 2).start()
    places = []
    for j in range(rows):
        core = (me + j // half) % 2
        owner = 2 * flipped(me // 2, core, j % half, half) + core
        distance = (owner // per_plane + cols - plane) % cols
        places.append(pl.multiple_of((distance * per_plane + owner % per_plane) * step, step))
    if not whole and given == rows:
        for piece, place in zip(pieces, places):
            left[pl.ds(place, step), :] = piece[0]
            right[pl.ds(place, step), :] = piece[1]
    elif not whole:
        some = block_of(depth, 512)

        def activate(i, carry):
            columns = pl.ds(pl.multiple_of(i * some, 128), some)
            for hidden_grad, saved, place in zip(pieces[:rows], pieces[rows:], places):
                gate_grad, up_grad = swiglu_back(
                    hidden_grad[:, columns].astype(jnp.float32),
                    saved[0, :, columns],
                    saved[1, :, columns],
                )
                left[pl.ds(place, step), columns] = gate_grad
                right[pl.ds(place, step), columns] = up_grad
            return carry

        lax.fori_loop(0, depth // some, activate, 0)

    def multiply(which, held, i):
        fetch(which, i).wait()
        product = contract_last(held[...], buffer[lax.rem(2 * i + which, SLOTS)])

        @pl.when(2 * i + which + SLOTS < 2 * steps)
        def _():
            fetch(which, i + SLOTS // 2).start()

        return product

    def body(i, carry):
        result = multiply(0, left, i) + multiply(1, right, i)
        columns = pl.ds(pl.multiple_of(i * block, 128), block)
        outs[0][:, columns] = result[:count]
        for d in range(1, cols):
            outs[d][:, columns] = result[d * count : (d + 1) * count].astype(jnp.bfloat16)
        return carry

    lax.fori_loop(0, steps, body, 0)


def input_partial(rows, cols, given, gate_weight, up_weight, start, size):
    step, depth = given[0].shape[-2:]
    if len(given) == 2:
        step //= rows
    count = step * rows // cols
    block = block_of(size, 256)
    whole, anywhere = pl.BlockSpec(memory_space=pltpu.VMEM), pl.BlockSpec(memory_space=pl.ANY)
    outs = (jax.ShapeDtypeStruct((count, size), jnp.float32),)
    outs += (jax.ShapeDtypeStruct((count, size), jnp.bfloat16),) * (cols - 1)
    if len(given) > 2:
        outs += (jax.ShapeDtypeStruct((rows * step, depth), jnp.bfloat16),) * 2
    outs = pl.pallas_call(
        functools.partial(input_kernel, rows, cols, start, block),
        out_shape=outs,
        in_specs=[whole] * len(given) + [anywhere] * 2,
        out_specs=(whole,) * len(outs),
        scratch_shapes=[
            pltpu.VMEM((SLOTS, block, depth), jnp.bfloat16),
            pltpu.SemaphoreType.DMA((SLOTS,)),
        ],
        compiler_params=pltpu.CompilerParams(vmem_limit_bytes=30 * MIB),
        cost_estimate=pl.CostEstimate(flops=HINT, bytes_accessed=HINT, transcendentals=0),
    )(*given, gate_weight, up_weight)
    return outs[:cols], outs[cols:]


class Chain:
    def __init__(self):
        self.last = []

    def begin(self, value):
        return after(value, *self.last) if self.last else value

    def end(self, *values):
        self.last = list(values)


class Halving:
    def __init__(self, chain, rows, send, keep):
        self.chain, self.rows, self.keep = chain, rows, keep
        self.got, self.step = swap(send, rows), 0

    def pair(self):
        got = self.chain.begin(self.got)
        pair = self.keep + got.astype(jnp.float32)
        self.state = {k: pair[k] for k in range(pair.shape[0])}
        self.send()

    def send(self):
        self.sent = [k for k in sorted(self.state) if (k >> self.step) & 1]
        value = jnp.stack([self.state[k] for k in self.sent]).astype(jnp.bfloat16)
        self.chain.end(value)
        self.got = exchange(value, self.rows, self.step)

    def add(self):
        got = self.chain.begin(self.got)
        for j, k in enumerate(self.sent):
            to = k ^ (1 << self.step)
            self.state[to] = self.state[to] + got[j].astype(jnp.float32)
            del self.state[k]
        self.step += 1


def per_device(rows, cols, out_grad, gate_saved, up_saved, gate_weight, up_weight, down_weight):
    share, hidden = gate_saved.shape
    width = out_grad.shape[1]
    per_plane = rows // cols
    step = share // TOKEN_CHUNKS
    mid = hidden // 2
    half = rows // 2
    bits = range(half.bit_length() - 1)
    chain = Chain()

    def tokens(t):
        own = out_grad.reshape(per_plane, TOKEN_CHUNKS, step, width)[:, t]
        return own.reshape(per_plane * step, width)

    def multiply(pieces, parts):
        pieces = [chain.begin(pieces[0])] + pieces[1:]
        outs = hidden_partial(rows, cols, pieces, down_weight, [i * mid for i in parts], mid)
        chain.end(outs[1])
        return [
            Halving(chain, rows, *outs[2 * n : 2 * n + 2]) for n in range(len(parts))
        ]

    def next_sums(sides):
        for side in sides:
            side.add()
            side.send()

    def own_hidden(sides):
        for side in sides:
            side.add()
        return jnp.concatenate([side.state[0] for side in sides], axis=1)

    def saved(t):
        mine = slice(t * step, (t + 1) * step)
        return gate_saved[mine], up_saved[mine]

    def spread(pieces):
        j = len(pieces).bit_length() - 1
        return pieces + [exchange(piece, rows, j) for piece in pieces]

    def cross(pieces):
        return pieces + [swap(piece, rows) for piece in pieces]

    def share_of(given, start, size):
        given = [chain.begin(given[0])] + list(given[1:])
        outs, both = input_partial(rows, cols, given, gate_weight, up_weight, start, size)
        chain.end(outs[0])
        return outs, both

    def start_sums(own, *sends):
        return [own] + [turn(send, cols, d) for d, send in enumerate(sends, 1)]

    def add_up(own, *others):
        own = chain.begin(own)
        for other in others:
            own = own + other.astype(jnp.float32)
        chain.end(own)
        return own

    own, later = tokens(0), tokens(1)
    near = [own] + [turn(own, cols, d) for d in range(1, cols)]
    later = after(later, near[1])
    far = [later] + [turn(later, cols, d) for d in range(1, cols)]

    known = [jnp.stack(saved(0))]
    for _ in bits[1:]:
        known = spread(known)
    chain.end(*known[1:])
    first = multiply(near, [0])
    known = spread(known)
    chain.last += known[1:]
    first += multiply(near, [1])
    known = cross(known)
    for side in first:
        side.pair()
    chain.last += known[1:]
    for _ in bits[1:]:
        next_sums(first)
    second = multiply(far, [0])
    first = [own_hidden(first).astype(jnp.bfloat16)]
    chain.end(first[0])
    for _ in bits:
        first = spread(first)
    second += multiply(far, [1])
    for side in second:
        side.pair()
    for _ in bits[1:]:
        next_sums(second)
    chain.last += first[1:]
    second = [jnp.stack(swiglu_back(own_hidden(second), *saved(1)))]
    chain.end(second[0])
    for _ in bits[1:]:
        second = spread(second)
    first = cross(first)
    sums, both = share_of(first + known, 0, width // 2)
    second = [chain.begin(piece) if j else piece for j, piece in enumerate(second)]
    second = spread(second)
    rest, _ = share_of(both, width // 2, width // 2)
    first = start_sums(*[jnp.concatenate(some, axis=1) for some in zip(sums, rest)])
    second = cross(second)
    sums, _ = share_of(second, 0, width)
    first = add_up(*first).astype(jnp.bfloat16)
    second = add_up(*start_sums(*sums)).astype(jnp.bfloat16)
    results = [value.reshape(per_plane, step, width) for value in (first, second)]
    return jnp.stack(results, axis=1).reshape(out_grad.shape)


def solution(mesh):
    rows, cols = mesh.shape["row"], mesh.shape["col"]
    placed = (
        P("col", "row"),
        P("row", "col"),
        P("row", "col"),
        P("row", "col"),
        P("row", "col"),
        P("col", "row"),
    )
    return jax.shard_map(
        functools.partial(per_device, rows, cols),
        mesh=mesh,
        in_specs=placed,
        out_specs=P("col", "row"),
        check_vma=False,
    )
```

```python
import functools

import jax
import jax.numpy as jnp
from jax import lax
from jax.experimental import pallas as pl
from jax.experimental.pallas import tpu as pltpu
from jax.sharding import PartitionSpec as P

TOKEN_CHUNKS = 2
SLOTS = 4
HINT = 1 << 10
MIB = 1 << 20


def contract_last(left, right):
    return lax.dot_general(
        left, right, (((1,), (1,)), ((), ())), preferred_element_type=jnp.float32
    )


def swiglu_back(hidden_grad, gate_saved, up_saved):
    gate_float = gate_saved.astype(jnp.float32)
    up_float = up_saved.astype(jnp.float32)
    sigmoid_gate = jax.nn.sigmoid(gate_float)
    up_grad = (hidden_grad * gate_float * sigmoid_gate).astype(jnp.bfloat16)
    gate_grad = (
        hidden_grad * up_float * sigmoid_gate * (1.0 + gate_float * (1.0 - sigmoid_gate))
    ).astype(jnp.bfloat16)
    return (gate_grad, up_grad)


def swap(value, size):
    return lax.ppermute(value, "row", [(i, i ^ 1) for i in range(size)])


def exchange(value, size, j):
    top = (size // 2).bit_length() - 2
    return lax.ppermute(
        value, "row", [(i, i ^ (2 << (top - j if i & 1 else j))) for i in range(size)]
    )


def turn(value, size, distance):
    return lax.ppermute(value, "col", [(i, (i + distance) % size) for i in range(size)])


def after(value, *earlier):
    return lax.optimization_barrier((value, *earlier))[0]


def flipped(chip, core, k, chips):
    other = 0
    count = chips.bit_length() - 1
    for i in range(count):
        flip = ((k >> i) & 1) + core * (((k >> (count - 1 - i)) & 1) - ((k >> i) & 1))
        other = other + ((chip // (1 << i)) % 2 + flip) % 2 * (1 << i)
    return other


def difference(chip, other, core, chips):
    k = 0
    count = chips.bit_length() - 1
    for i in range(count):
        differs = ((chip // (1 << i)) % 2 + (other // (1 << i)) % 2) % 2
        k = k + differs * ((1 << i) + core * ((1 << (count - 1 - i)) - (1 << i)))
    return k


def block_of(extent, most):
    return max(d for d in range(128, most + 1, 128) if extent % d == 0)


def hidden_kernel(rows, cols, starts, block, count, *refs):
    pieces, weight, refs = refs[:count], refs[count], refs[count + 1 :]
    outs, (tokens, buffer, sems) = refs[:-3], refs[-3:]
    me, plane = lax.axis_index("row"), lax.axis_index("col")
    per_plane, half = rows // cols, rows // 2
    step = outs[0].shape[1]
    steps = outs[0].shape[2] // block

    def fetch(start, i):
        slot = lax.rem(i, SLOTS)
        return pltpu.make_async_copy(
            weight.at[pl.ds(start + i * block, block)], buffer.at[slot], sems.at[slot]
        )

    for i in range(min(SLOTS, steps)):
        fetch(starts[0], i).start()

    def place(piece, owner_plane):
        for sub in range(per_plane):
            owner = owner_plane * per_plane + sub
            k = difference(me // 2, owner // 2, owner % 2, half)
            same = 1 - (owner % 2 + me % 2) % 2
            to = pl.multiple_of((same * half + k) * step, step)
            tokens[pl.ds(to, step), :] = piece[sub * step : (sub + 1) * step, :]

    place(pieces[0], plane)
    for d in range(1, cols):
        if count == cols:
            place(pieces[d], (plane + cols - d) % cols)
        else:
            pl.when(plane >= d)(functools.partial(place, pieces[d], plane - d))
            pl.when(plane + d < cols)(functools.partial(place, pieces[cols - 1 + d], plane + d))

    for n, start in enumerate(starts):
        send, keep = outs[2 * n : 2 * n + 2]
        if n:
            for i in range(min(SLOTS, steps)):
                fetch(start, i).start()

        def body(i, carry):
            fetch(start, i).wait()
            result = contract_last(tokens[...], buffer[lax.rem(i, SLOTS)])
            columns = pl.ds(pl.multiple_of(i * block, 128), block)
            for k in range(half):
                send[k, :, columns] = result[k * step : (k + 1) * step].astype(send.dtype)
                keep[k, :, columns] = result[(half + k) * step : (half + k + 1) * step]

            @pl.when(i + SLOTS < steps)
            def _():
                fetch(start, i + SLOTS).start()

            return carry

        lax.fori_loop(0, steps, body, 0)


def hidden_partial(rows, cols, pieces, weight, starts, size):
    count, width = pieces[0].shape
    step = count * cols // rows
    half = rows // 2
    block = block_of(size, 256)
    whole = pl.BlockSpec(memory_space=pltpu.VMEM)
    return pl.pallas_call(
        functools.partial(hidden_kernel, rows, cols, starts, block, len(pieces)),
        out_shape=(
            jax.ShapeDtypeStruct((half, step, size), jnp.bfloat16),
            jax.ShapeDtypeStruct((half, step, size), jnp.float32),
        )
        * len(starts),
        in_specs=[whole] * len(pieces) + [pl.BlockSpec(memory_space=pl.ANY)],
        out_specs=(whole,) * (2 * len(starts)),
        scratch_shapes=[
            pltpu.VMEM((rows * step, width), jnp.bfloat16),
            pltpu.VMEM((SLOTS, block, width), jnp.bfloat16),
            pltpu.SemaphoreType.DMA((SLOTS,)),
        ],
        compiler_params=pltpu.CompilerParams(vmem_limit_bytes=30 * MIB),
        cost_estimate=pl.CostEstimate(flops=HINT, bytes_accessed=HINT, transcendentals=0),
    )(*pieces, weight)


def input_kernel(rows, cols, start, block, *refs):
    refs, (buffer, sems) = refs[:-2], refs[-2:]
    given = len(refs) - 2 - cols
    whole = given == 2
    if whole:
        (left, right), refs = refs[:2], refs[2:]
    else:
        given -= 2
        pieces, refs, (left, right) = refs[:given], refs[given:-2], refs[-2:]
    (gate_weight, up_weight), outs = refs[:2], refs[2:]
    me, plane = lax.axis_index("row"), lax.axis_index("col")
    per_plane, half = rows // cols, rows // 2
    depth = left.shape[1]
    step = left.shape[0] // rows
    steps = outs[0].shape[1] // block
    count = per_plane * step

    def fetch(which, i):
        slot = lax.rem(2 * i + which, SLOTS)
        return pltpu.make_async_copy(
            (gate_weight, up_weight)[which].at[pl.ds(start + i * block, block)],
            buffer.at[slot],
            sems.at[slot],
        )

    for i in range(min(SLOTS, 2 * steps)):
        fetch(i % 2, i // 2).start()
    places = []
    for j in range(rows):
        core = (me + j // half) % 2
        owner = 2 * flipped(me // 2, core, j % half, half) + core
        distance = (owner // per_plane + cols - plane) % cols
        places.append(pl.multiple_of((distance * per_plane + owner % per_plane) * step, step))
    if not whole and given == rows:
        for piece, place in zip(pieces, places):
            left[pl.ds(place, step), :] = piece[0]
            right[pl.ds(place, step), :] = piece[1]
    elif not whole:
        some = block_of(depth, 512)

        def activate(i, carry):
            columns = pl.ds(pl.multiple_of(i * some, 128), some)
            for hidden_grad, saved, place in zip(pieces[:rows], pieces[rows:], places):
                gate_grad, up_grad = swiglu_back(
                    hidden_grad[:, columns].astype(jnp.float32),
                    saved[0, :, columns],
                    saved[1, :, columns],
                )
                left[pl.ds(place, step), columns] = gate_grad
                right[pl.ds(place, step), columns] = up_grad
            return carry

        lax.fori_loop(0, depth // some, activate, 0)

    def multiply(which, held, i):
        fetch(which, i).wait()
        product = contract_last(held[...], buffer[lax.rem(2 * i + which, SLOTS)])

        @pl.when(2 * i + which + SLOTS < 2 * steps)
        def _():
            fetch(which, i + SLOTS // 2).start()

        return product

    def body(i, carry):
        result = multiply(0, left, i) + multiply(1, right, i)
        columns = pl.ds(pl.multiple_of(i * block, 128), block)
        outs[0][:, columns] = result[:count]
        for d in range(1, cols):
            outs[d][:, columns] = result[d * count : (d + 1) * count].astype(jnp.bfloat16)
        return carry

    lax.fori_loop(0, steps, body, 0)


def input_partial(rows, cols, given, gate_weight, up_weight, start, size):
    step, depth = given[0].shape[-2:]
    if len(given) == 2:
        step //= rows
    count = step * rows // cols
    block = block_of(size, 256)
    whole, anywhere = pl.BlockSpec(memory_space=pltpu.VMEM), pl.BlockSpec(memory_space=pl.ANY)
    outs = (jax.ShapeDtypeStruct((count, size), jnp.float32),)
    outs += (jax.ShapeDtypeStruct((count, size), jnp.bfloat16),) * (cols - 1)
    if len(given) > 2:
        outs += (jax.ShapeDtypeStruct((rows * step, depth), jnp.bfloat16),) * 2
    outs = pl.pallas_call(
        functools.partial(input_kernel, rows, cols, start, block),
        out_shape=outs,
        in_specs=[whole] * len(given) + [anywhere] * 2,
        out_specs=(whole,) * len(outs),
        scratch_shapes=[
            pltpu.VMEM((SLOTS, block, depth), jnp.bfloat16),
            pltpu.SemaphoreType.DMA((SLOTS,)),
        ],
        compiler_params=pltpu.CompilerParams(vmem_limit_bytes=30 * MIB),
        cost_estimate=pl.CostEstimate(flops=HINT, bytes_accessed=HINT, transcendentals=0),
    )(*given, gate_weight, up_weight)
    return outs[:cols], outs[cols:]


class Chain:
    def __init__(self):
        self.last = []

    def begin(self, value):
        return after(value, *self.last) if self.last else value

    def end(self, *values):
        self.last = list(values)


class Halving:
    def __init__(self, chain, rows, send, keep):
        self.chain, self.rows, self.keep = chain, rows, keep
        self.got, self.step = swap(send, rows), 0

    def pair(self):
        got = self.chain.begin(self.got)
        pair = self.keep + got.astype(jnp.float32)
        self.state = {k: pair[k] for k in range(pair.shape[0])}
        self.send()

    def send(self):
        self.sent = [k for k in sorted(self.state) if (k >> self.step) & 1]
        value = jnp.stack([self.state[k] for k in self.sent]).astype(jnp.bfloat16)
        self.chain.end(value)
        self.got = exchange(value, self.rows, self.step)

    def add(self):
        got = self.chain.begin(self.got)
        for j, k in enumerate(self.sent):
            to = k ^ (1 << self.step)
            self.state[to] = self.state[to] + got[j].astype(jnp.float32)
            del self.state[k]
        self.step += 1


def per_device(rows, cols, out_grad, gate_saved, up_saved, gate_weight, up_weight, down_weight):
    share, hidden = gate_saved.shape
    width = out_grad.shape[1]
    per_plane = rows // cols
    step = share // TOKEN_CHUNKS
    mid = hidden // 2
    half = rows // 2
    bits = range(half.bit_length() - 1)
    chain = Chain()

    def tokens(t):
        own = out_grad.reshape(per_plane, TOKEN_CHUNKS, step, width)[:, t]
        return own.reshape(per_plane * step, width)

    def multiply(pieces, parts):
        pieces = [chain.begin(pieces[0])] + pieces[1:]
        outs = hidden_partial(rows, cols, pieces, down_weight, [i * mid for i in parts], mid)
        chain.end(outs[1])
        return [
            Halving(chain, rows, *outs[2 * n : 2 * n + 2]) for n in range(len(parts))
        ]

    def next_sums(sides):
        for side in sides:
            side.add()
            side.send()

    def own_hidden(sides):
        for side in sides:
            side.add()
        return jnp.concatenate([side.state[0] for side in sides], axis=1)

    def saved(t):
        mine = slice(t * step, (t + 1) * step)
        return gate_saved[mine], up_saved[mine]

    def spread(pieces):
        j = len(pieces).bit_length() - 1
        return pieces + [exchange(piece, rows, j) for piece in pieces]

    def cross(pieces):
        return pieces + [swap(piece, rows) for piece in pieces]

    def share_of(given, start, size):
        given = [chain.begin(given[0])] + list(given[1:])
        outs, both = input_partial(rows, cols, given, gate_weight, up_weight, start, size)
        chain.end(outs[0])
        return outs, both

    def start_sums(own, *sends):
        return [own] + [turn(send, cols, d) for d, send in enumerate(sends, 1)]

    def add_up(own, *others):
        own = chain.begin(own)
        for other in others:
            own = own + other.astype(jnp.float32)
        chain.end(own)
        return own

    own, later = tokens(0), tokens(1)
    near = [own] + [turn(own, cols, d) for d in range(1, cols)]
    later = after(later, near[1])
    far = [later] + [turn(later, cols, d) for d in range(1, cols)]

    known = [jnp.stack(saved(0))]
    for _ in bits[1:]:
        known = spread(known)
    chain.end(*known[1:])
    first = multiply(near, [0])
    known = spread(known)
    first += multiply(near, [1])
    chain.last += known[1:]
    known = cross(known)
    for side in first:
        side.pair()
    chain.last += known[1:]
    for _ in bits[1:]:
        next_sums(first)
    first = [own_hidden(first).astype(jnp.bfloat16)]
    chain.end(first[0])
    for _ in bits[1:]:
        first = spread(first)
    second = multiply(far, [0])
    chain.last += first[1:]
    first = spread(first)
    second += multiply(far, [1])
    for side in second:
        side.pair()
    for _ in bits[1:]:
        next_sums(second)
    chain.last += first[1:]
    second = [jnp.stack(swiglu_back(own_hidden(second), *saved(1)))]
    chain.end(second[0])
    for _ in bits[1:]:
        second = spread(second)
    first = cross(first)
    sums, both = share_of(first + known, 0, width // 2)
    second = [chain.begin(piece) if j else piece for j, piece in enumerate(second)]
    second = spread(second)
    rest, _ = share_of(both, width // 2, width // 2)
    first = start_sums(*[jnp.concatenate(some, axis=1) for some in zip(sums, rest)])
    second = cross(second)
    sums, _ = share_of(second, 0, width)
    first = add_up(*first).astype(jnp.bfloat16)
    second = add_up(*start_sums(*sums)).astype(jnp.bfloat16)
    results = [value.reshape(per_plane, step, width) for value in (first, second)]
    return jnp.stack(results, axis=1).reshape(out_grad.shape)


def solution(mesh):
    rows, cols = mesh.shape["row"], mesh.shape["col"]
    placed = (
        P("col", "row"),
        P("row", "col"),
        P("row", "col"),
        P("row", "col"),
        P("row", "col"),
        P("col", "row"),
    )
    return jax.shard_map(
        functools.partial(per_device, rows, cols),
        mesh=mesh,
        in_specs=placed,
        out_specs=P("col", "row"),
        check_vma=False,
    )
```
